32 devices in a mesh: groups: 2 (over x), tm: 16 (over z, y, core).
Axes of the slice: x: 2, y: 2, z: 4, core: 2. Of those that a mesh axis runs over, the one named last changes fastest.
Arguments:
- new_rows: bfloat16 [16384, 2048], P(('groups', 'tm')), parts along dimension 0, may hold values from -6 to 6
- w_query: bfloat16 [2048, 1024], replicated, may hold values from -0.125 to 0.125
- w_out: bfloat16 [1024, 2048], replicated, may hold values from -1.5 to 1.5
- base_kv: bfloat16 [2, 128, 128, 1024], P(None, ('groups', 'tm')), parts along dimension 1, may hold values from -1400 to 1400
- slopes: float32 [8], replicated, may hold values from 0.05 to 2
- row_owner: int32 [16384, 1], P(('groups', 'tm')), parts along dimension 0, may hold values from 0 to 15; in each aligned block of 512 rows (0 to 511, 512 to 1023, ...) at most 64 rows name the same one
- row_position: int32 [16384], P(('groups', 'tm')), parts along dimension 0, may hold values from 0 to 11
- row_reach: int32 [16384, 2], P(('groups', 'tm')), parts along dimension 0, may hold values from 0 to 2
Outputs:
- upsampled: bfloat16 [16384, 2048], P(('groups', 'tm')), parts along dimension 0
The draws below stay inside these ranges and needn't reach their ends.
There are 2 independent parts, one for each index of `groups`. The reference program is written for one: setup_inputs(seed, part) draws one part's arguments, and reference() takes and returns one part's arrays. A program takes and returns all parts, laid end to end along the dimension named above; an argument that names none is the same for every part. Nothing has to cross between parts.
Inputs may be any that keep to these rules, and one draw needn't show every extreme that they name: `row_owner`: in the rows of one time block no owner is named by more than 64 rows, a bound that some block reaches.
All inputs are finite; a program needn't handle non-finite values.
Results may differ from the reference program's by a relative error of at most 0.01.
The reference program's roundings to bfloat16 on the way (of `queries`, `weights` and `attended`) count: a program that leaves them out, or rounds other values in their place, can miss the bound.
Values may be sent and summed in bfloat16 or wider, within the bound.
A program may use at most 128 MiB of HBM per device.

```python
import math
import jax
import jax.numpy as jnp
import numpy as np
from jax import lax

D = 2048
HEADS = 8
HEAD_DIM = 128
REACH = 2
BF = 4
P_SIZE = 128
R_DEV = 512
HQ = 1024
CAP = 64
BASE = 64
ROWS = 8192
N_TM = 16


def draw_base_kv(key, part):
    key = jax.random.fold_in(key, 7)
    shape = (2, BASE, P_SIZE, HQ)
    values = jnp.clip(jax.random.normal(key, shape, jnp.float32), -6.0, 6.0)
    return values.astype(jnp.bfloat16)


def touch_ends(drawn, own_key, smallest, high):
    shape = drawn.shape
    spot = [jax.random.randint(jax.random.fold_in(own_key, axis), (), 0, shape[axis]) for axis in range(len(shape))]
    drawn = drawn.at[tuple(spot)].set(smallest)
    longest = shape.index(max(shape))
    spot[longest] = (spot[longest] + 1) % shape[longest]
    return drawn.at[tuple(spot)].set(high)


def steps_of(rng, extent, pieces, low, high):
    level, own = 1.0, jax.random.fold_in(rng, 6)
    for dim, parts in pieces:
        steps = jnp.exp(jax.random.uniform(jax.random.fold_in(own, dim), (parts,), jnp.float32, low / len(pieces), high / len(pieces)))
        level = level * jnp.repeat(steps, extent[dim] // parts).reshape([-1 if axis == dim else 1 for axis in range(len(extent))])
    return level


def deal_out(key, own, number, rows, number_of, top, reach, slope):
    order = jax.random.permutation(key, number_of)
    crowded, usual = load_shares(number_of, rows * top, reach, slope, True), load_shares(number_of, rows * top, reach, slope, False)
    places = jnp.arange(number_of)

    def named(tallies, turn):
        used = int((tallies > 0).sum())
        fixed = max(1, used // 4)
        passed = fixed + (places - fixed + turn * (used - fixed)) % max(1, number_of - fixed)
        return jnp.zeros((number_of,), jnp.int32).at[order[jnp.where(places < fixed, places, passed)]].set(jnp.asarray(tallies, jnp.int32))

    tallies = jnp.where(number % 4 == 0, named(crowded, number // 4), named(usual, number - number // 4 - 1))
    mixed = jax.random.permutation(jax.random.fold_in(own, 3), number_of)
    giver, taker = mixed[0:number_of // 2 * 2:2], mixed[1:number_of // 2 * 2:2]
    slack = jnp.minimum(tallies[giver] - 1, reach - tallies[taker]) // 2
    slack = jnp.where((giver == order[0]) | (taker == order[0]) | (tallies[taker] == 0), 0, jnp.maximum(slack, 0))
    passed = jax.random.randint(jax.random.fold_in(own, 4), (number_of // 2,), 0, 1 << 20) % (slack + 1)
    tallies = tallies.at[giver].add(-passed).at[taker].add(passed)
    labels = jnp.searchsorted(jnp.cumsum(tallies), jnp.arange(rows * top), side="right").astype(jnp.int32)
    grid = labels.reshape(top, rows).T
    grid = grid[jax.random.permutation(jax.random.fold_in(own, 1), rows)]
    turn = jax.random.randint(jax.random.fold_in(own, 2), (rows, 1), 0, top)
    return jnp.take_along_axis(grid, (jnp.arange(top)[None, :] + turn) % top, axis=1)


def load_shares(amount, total, most, lean, full):
    weights = [(1 << 20) // math.isqrt(grade ** lean) + 1 for grade in range(1, amount + 1)]
    largest = most if full else min(most, max(-(-total // amount), total * weights[0] // sum(weights)))
    least = 1 if total - largest >= amount - 1 else 0
    given, surplus = [largest] + [least] * (amount - 1), total - largest - least * (amount - 1)
    while surplus > 0:
        candidates = [i for i in range(1, amount) if given[i] < largest] or [i for i in range(1, amount) if given[i] < most]
        whole, budget = sum([weights[i] for i in candidates]), surplus
        for i in candidates:
            addition = min(most - given[i], max(1, budget * weights[i] // whole), surplus)
            given[i] = given[i] + addition
            surplus = surplus - addition
    return np.array(given)


def centred(key, dims, spread, reach, pieces=(), kind=jnp.bfloat16):
    array = jax.random.normal(key, dims, jnp.float32) * spread
    if len(pieces) > 0:
        array = steps_of(key, dims, pieces, -0.22, 0.18) * array
    return jnp.clip(array, min=-reach, max=reach).astype(kind)


def setup_inputs(seed: int = 0, part: int = 0) -> dict:
    splits = jax.random.split(jax.random.key(seed), 9)
    part_keys = jax.random.split(jax.random.fold_in(splits[8], part), 9)
    new_rows = centred(part_keys[0], (ROWS, D), 1.0, 6.0, ((0, 16),))
    w_query = centred(splits[1], (D, HQ), D ** -0.5, 0.125)
    w_out = centred(splits[2], (HQ, D), 0.25, 1.5)
    base_kv = draw_base_kv(jax.random.fold_in(jax.random.fold_in(splits[8], part), 71), part)
    slopes = jnp.clip(jnp.exp(jax.random.uniform(splits[4], (HEADS,), jnp.float32, math.log(0.05), math.log(2.0))), 0.05, 2.0)
    row_owner_keys = jax.random.split(jax.random.fold_in(part_keys[5], 1), ROWS // R_DEV)
    row_owner_turns = jax.random.permutation(jax.random.fold_in(part_keys[5], 3), ROWS // R_DEV)
    row_owner = jax.vmap(lambda own, number: deal_out(jax.random.fold_in(part_keys[5], 2), own, number, R_DEV, N_TM, 1, CAP, 2))(row_owner_keys, row_owner_turns).reshape((ROWS, 1))
    row_position = touch_ends(jax.random.randint(part_keys[6], (ROWS,), 0, 3 * BF), jax.random.fold_in(part_keys[6], 1), 0, (3 * BF) - 1).astype(jnp.int32)
    row_reach = touch_ends(jax.random.randint(part_keys[7], (ROWS, 2), 0, REACH + 1), jax.random.fold_in(part_keys[7], 1), 0, REACH).astype(jnp.int32)
    return dict(new_rows=new_rows, w_query=w_query, w_out=w_out, base_kv=base_kv, slopes=slopes, row_owner=row_owner, row_position=row_position, row_reach=row_reach)


def attend(queries, details, extended, slopes, first_frame, total_frames):
    slots = queries.shape[0]
    frames = extended.shape[1]
    tile = extended.shape[2]
    position = details[:, 0]
    centre = first_frame + REACH + position // 3
    moment = centre.astype(jnp.float32) + ((position % 3) + 1).astype(jnp.float32) * 0.25
    key_frame = jnp.repeat(first_frame + jnp.arange(frames, dtype=jnp.int32), tile)
    allowed = (key_frame[None, :] >= (centre - details[:, 1])[:, None]) & (key_frame[None, :] <= (centre + details[:, 2])[:, None])
    allowed = allowed & (key_frame >= 0)[None, :] & (key_frame < total_frames)[None, :]
    distance = jnp.abs(key_frame.astype(jnp.float32)[None, None, :] - moment[None, :, None])
    query_heads = queries.reshape(slots, HEADS, HEAD_DIM).astype(jnp.float32)
    key_heads = extended[0].reshape(frames * tile, HEADS, HEAD_DIM).astype(jnp.float32)
    value_heads = extended[1].reshape(frames * tile, HEADS, HEAD_DIM).astype(jnp.float32)
    scores = jnp.einsum("shd,khd->hsk", query_heads, key_heads) * (1.0 / HEAD_DIM ** 0.5)
    scores = scores - slopes[:, None, None] * distance
    scores = jnp.where(allowed[None], scores, -1e30)
    largest = jnp.max(scores, axis=-1, keepdims=True)
    raised = jnp.exp(scores - largest)
    weights = (raised / jnp.sum(raised, axis=-1, keepdims=True)).astype(jnp.bfloat16)
    attended = jnp.einsum("hsk,khd->shd", weights.astype(jnp.float32), value_heads)
    return attended.reshape(slots, HEADS * HEAD_DIM).astype(jnp.bfloat16)


def reference(new_rows, w_query, w_out, base_kv, slopes, row_owner, row_position, row_reach):
    queries = jnp.dot(new_rows, w_query, preferred_element_type=jnp.float32).astype(jnp.bfloat16)
    owner = row_owner[:, 0]
    owner_block = owner.reshape(N_TM, R_DEV)
    owner_hits = (owner_block[:, :, None] == jnp.arange(N_TM, dtype=jnp.int32)[None, None, :]).astype(jnp.int32)
    owner_rank = jnp.cumsum(owner_hits, axis=1) - 1
    slot_index = jnp.sum(owner_hits * owner_rank, axis=-1)
    sources = jnp.arange(N_TM, dtype=jnp.int32)[:, None]
    column = (sources * CAP + slot_index).reshape(ROWS).astype(jnp.int32)
    table = jnp.full((N_TM, N_TM * CAP), ROWS, jnp.int32).at[owner, column].set(jnp.arange(ROWS, dtype=jnp.int32))
    row_info = jnp.stack([row_position, row_reach[:, 0], row_reach[:, 1]], axis=1).astype(jnp.int32)
    padded_queries = jnp.concatenate([queries, jnp.zeros((1, HQ), jnp.bfloat16)], axis=0)
    padded_info = jnp.concatenate([row_info, jnp.zeros((1, 3), jnp.int32)], axis=0)
    padded_kv = jnp.pad(base_kv, ((0, 0), (REACH, REACH), (0, 0), (0, 0)))

    def per_owner(owner_index):
        picked = table[owner_index]
        extended = lax.dynamic_slice_in_dim(padded_kv, owner_index * BF, BF + 2 * REACH, axis=1)
        return attend(padded_queries[picked], padded_info[picked], extended, slopes, owner_index * BF - REACH, BASE)

    results = lax.map(per_owner, jnp.arange(N_TM, dtype=jnp.int32))
    gathered = results[owner, column]
    return jnp.dot(gathered, w_out, preferred_element_type=jnp.float32).astype(jnp.bfloat16)
```

```python
import functools

import jax
import jax.numpy as jnp
from jax import lax
from jax.experimental import pallas as pl
from jax.experimental.pallas import tpu as pltpu
from jax.sharding import PartitionSpec as P

HEAD_DIM = 128
REACH = 2
CHUNK = 128
MESH = pl.DeviceIdType.MESH
F32 = jnp.float32
BF16 = jnp.bfloat16


def iota(shape, axis):
    return lax.broadcasted_iota(jnp.int32, shape, axis)


def kernel(
    n, slopes_ref, info_ref, x_hbm, wq_hbm, wo_hbm, kv_hbm, out_ref,
    x, wq, wo, ext, queries, q_slots, q_recv, m_slots, m_recv, att, ret, vt, gather,
    load_sem, halo_send, halo_recv, qs_sem, qr_sem, ms_sem, mr_sem, rs_sem, rr_sem,
):
    me = lax.axis_index("tm")
    rows = x.shape[0]
    slots = q_slots.shape[0]
    cap = slots // n
    group = CHUNK // cap
    chunks = slots // CHUNK
    half = chunks // 2
    frames = kv_hbm.shape[1]
    wide = frames + 2 * REACH
    tokens = kv_hbm.shape[2]
    heads = queries.shape[1] // HEAD_DIM
    own = lax.div(me, group)
    own_half = lax.div(own, half)
    own_spot = lax.rem(own, half)

    loads = [
        pltpu.make_async_copy(kv_hbm, ext.at[:, REACH:REACH + frames], load_sem.at[0]),
        pltpu.make_async_copy(x_hbm, x, load_sem.at[1]),
        pltpu.make_async_copy(wq_hbm, wq, load_sem.at[2]),
        pltpu.make_async_copy(wo_hbm, wo, load_sem.at[3]),
    ]
    for load in loads:
        load.start()

    barrier = pltpu.get_barrier_semaphore()

    @pl.loop(1, n)
    def _(k):
        pl.semaphore_signal(
            barrier, inc=1, device_id={"tm": lax.rem(me + k, n)}, device_id_type=MESH
        )

    pl.semaphore_wait(barrier, n - 1)

    to_right = pltpu.make_async_remote_copy(
        src_ref=kv_hbm.at[:, frames - REACH:], dst_ref=ext.at[:, :REACH],
        send_sem=halo_send.at[0], recv_sem=halo_recv.at[0],
        device_id={"tm": lax.rem(me + 1, n)}, device_id_type=MESH,
    )
    to_left = pltpu.make_async_remote_copy(
        src_ref=kv_hbm.at[:, :REACH], dst_ref=ext.at[:, REACH + frames:],
        send_sem=halo_send.at[1], recv_sem=halo_recv.at[1],
        device_id={"tm": lax.rem(me + n - 1, n)}, device_id_type=MESH,
    )

    @pl.when(me < n - 1)
    def _():
        to_right.start()

    @pl.when(me > 0)
    def _():
        to_left.start()

    edge = jnp.zeros((2, REACH, tokens, ext.shape[3]), BF16)

    @pl.when(me == 0)
    def _():
        ext[:, :REACH] = edge

    @pl.when(me == n - 1)
    def _():
        ext[:, REACH + frames:] = edge

    info = info_ref[...]
    owner = info[0:1]
    hits = (owner == iota((n, rows), 0).astype(F32)).astype(F32)
    upper = (iota((rows, rows), 0) <= iota((rows, rows), 1)).astype(F32).astype(BF16)
    counts = jnp.dot(hits.astype(BF16), upper, preferred_element_type=F32)
    rank = jnp.sum(hits * counts, axis=0, keepdims=True) - 1.0
    slot = owner * float(cap) + rank
    slot_column = jnp.sum(
        jnp.where(iota((rows, rows), 0) == iota((rows, rows), 1), slot, 0.0), axis=1, keepdims=True
    )
    gather[...] = (slot_column == iota((rows, slots), 1).astype(F32)).astype(F32).astype(BF16)
    facts = info.astype(BF16)
    spot = rank + (lax.rem(me, group) * cap).astype(F32)

    loads[1].wait()
    loads[2].wait()

    @pl.loop(0, queries.shape[1] // 256)
    def _(j):
        columns = pl.ds(pl.multiple_of(j * 256, 256), 256)
        queries[:, columns] = jnp.dot(x[...], wq[:, columns], preferred_element_type=F32).astype(BF16)

    def q_copy(target, source):
        return pltpu.make_async_remote_copy(
            src_ref=q_slots.at[pl.ds(pl.multiple_of(target * cap, cap), cap)],
            dst_ref=q_recv.at[pl.ds(pl.multiple_of(source * cap, cap), cap)],
            send_sem=qs_sem.at[target], recv_sem=qr_sem.at[source],
            device_id={"tm": target}, device_id_type=MESH,
        )

    def m_copy(target, source):
        return pltpu.make_async_remote_copy(
            src_ref=m_slots.at[target], dst_ref=m_recv.at[source],
            send_sem=ms_sem.at[target], recv_sem=mr_sem.at[source],
            device_id={"tm": target}, device_id_type=MESH,
        )

    def r_copy(target, source):
        return pltpu.make_async_remote_copy(
            src_ref=att.at[pl.ds(pl.multiple_of(target * cap, cap), cap)],
            dst_ref=ret.at[pl.ds(pl.multiple_of(source * cap, cap), cap)],
            send_sem=rs_sem.at[target], recv_sem=rr_sem.at[source],
            device_id={"tm": target}, device_id_type=MESH,
        )

    mine = pl.ds(pl.multiple_of(me * cap, cap), cap)

    @pl.loop(0, chunks)
    def _(i):
        side = lax.rem(own_half + 1 + lax.rem(i, 2), 2)
        chunk = side * half + lax.rem(own_spot + lax.div(i, 2), half)
        first = (chunk * CHUNK).astype(F32)
        place = (slot - first == iota((CHUNK, rows), 0).astype(F32)).astype(F32).astype(BF16)

        @pl.loop(0, queries.shape[1] // 256)
        def _(j):
            columns = pl.ds(pl.multiple_of(j * 256, 256), 256)
            q_slots[pl.ds(pl.multiple_of(chunk * CHUNK, CHUNK), CHUNK), columns] = jnp.dot(
                place, queries[:, columns], preferred_element_type=F32
            ).astype(BF16)

        @pl.loop(0, group)
        def _(g):
            target = chunk * group + g
            lanes = jnp.where(owner == target.astype(F32), spot, -1.0)
            spread = (lanes == iota((CHUNK, rows), 0).astype(F32)).astype(F32).astype(BF16)
            m_slots[target] = lax.dot_general(
                facts, spread, (((1,), (1,)), ((), ())), preferred_element_type=F32
            )

            @pl.when(target != me)
            def _():
                m_copy(target, me).start()
                q_copy(target, me).start()

            @pl.when(target == me)
            def _():
                m_recv[target] = m_slots[target]
                q_recv[mine] = q_slots[mine]

    def turn(f):
        @pl.loop(0, heads)
        def _(h):
            columns = pl.ds(pl.multiple_of(h * HEAD_DIM, HEAD_DIM), HEAD_DIM)
            vt[columns, pl.ds(pl.multiple_of(f * tokens, tokens), tokens)] = (
                ext[1, f, :, columns].astype(F32).T.astype(BF16)
            )

    loads[0].wait()

    @pl.loop(REACH, REACH + frames)
    def _(f):
        turn(f)

    @pl.when(me > 0)
    def _():
        to_right.wait_recv()

    @pl.when(me < n - 1)
    def _():
        to_left.wait_recv()

    @pl.loop(0, REACH)
    def _(f):
        turn(f)
        turn(REACH + frames + f)

    first_frame = (me * frames - REACH).astype(F32)

    @pl.loop(0, chunks)
    def _(i):
        side = lax.rem(own_half + lax.rem(i, 2), 2)
        chunk = side * half + lax.rem(own_spot + half - lax.div(i, 2), half)

        @pl.loop(0, group)
        def _(g):
            source = chunk * group + g

            @pl.when(source != me)
            def _():
                m_copy(me, source).wait_recv()
                q_copy(me, source).wait_recv()

        told = m_recv[chunk * group]
        for g in range(1, group):
            told = told + m_recv[chunk * group + g]
        position = told[1:2].astype(jnp.int32)
        ahead = lax.div(position, 3)
        centre = (ahead + REACH).astype(F32) + first_frame
        moment = centre + (position - 3 * ahead + 1).astype(F32) * 0.25
        frame = first_frame + iota((wide, CHUNK), 0).astype(F32)
        allowed = (frame >= centre - told[2:3]) & (frame <= centre + told[3:4])
        allowed = allowed & (frame >= 0.0) & (frame < float(frames * n))
        distance = jnp.abs(frame - moment)
        chunk_rows = pl.ds(pl.multiple_of(chunk * CHUNK, CHUNK), CHUNK)

        @pl.loop(0, heads)
        def _(h):
            columns = pl.ds(pl.multiple_of(h * HEAD_DIM, HEAD_DIM), HEAD_DIM)
            bias = jnp.where(allowed, -slopes_ref[h] * distance, -1e30)
            keys = ext[0, :, :, columns].reshape(wide * tokens, HEAD_DIM)
            scores = lax.dot_general(
                keys, q_recv[chunk_rows, columns], (((1,), (1,)), ((), ())),
                preferred_element_type=F32,
            )
            scores = scores.reshape(wide, tokens, CHUNK) * (1.0 / HEAD_DIM**0.5) + bias[:, None, :]
            largest = jnp.max(jnp.max(scores, axis=0), axis=0, keepdims=True)
            raised = jnp.exp(scores - largest[None])
            total = jnp.sum(jnp.sum(raised, axis=0), axis=0, keepdims=True)
            weights = (raised * (1.0 / total)[None]).astype(BF16).reshape(wide * tokens, CHUNK)
            attended = jnp.dot(vt[columns, :], weights, preferred_element_type=F32)
            att[chunk_rows, columns] = attended.T.astype(BF16)

        @pl.loop(0, group)
        def _(g):
            source = chunk * group + g

            @pl.when(source != me)
            def _():
                r_copy(source, me).start()

            @pl.when(source == me)
            def _():
                ret[mine] = att[mine]

    loads[3].wait()

    @pl.loop(1, n)
    def _(k):
        r_copy(me, lax.rem(me + k, n)).wait_recv()

    @pl.loop(0, queries.shape[1] // 256)
    def _(j):
        columns = pl.ds(pl.multiple_of(j * 256, 256), 256)
        queries[:, columns] = jnp.dot(
            gather[...], ret[:, columns], preferred_element_type=F32
        ).astype(BF16)

    @pl.loop(0, wo.shape[1] // 256)
    def _(j):
        columns = pl.ds(pl.multiple_of(j * 256, 256), 256)
        out_ref[:, columns] = jnp.dot(
            queries[...], wo[:, columns], preferred_element_type=F32
        ).astype(BF16)

    @pl.loop(1, n)
    def _(k):
        target = lax.rem(me + k, n)
        m_copy(target, me).wait_send()
        q_copy(target, me).wait_send()
        r_copy(target, me).wait_send()

    @pl.when(me < n - 1)
    def _():
        to_right.wait_send()

    @pl.when(me > 0)
    def _():
        to_left.wait_send()


def per_device(n, new_rows, w_query, w_out, base_kv, slopes, row_owner, row_position, row_reach):
    rows, width = new_rows.shape
    features = w_query.shape[1]
    slots = 2 * rows
    frames, tokens = base_kv.shape[1:3]
    wide = frames + 2 * REACH
    info = jnp.concatenate(
        [row_owner.T, row_position[None], row_reach.T, jnp.zeros((4, rows), jnp.int32)], axis=0
    ).astype(F32)
    anywhere = pl.BlockSpec(memory_space=pl.ANY)
    return pl.pallas_call(
        functools.partial(kernel, n),
        out_shape=jax.ShapeDtypeStruct((rows, w_out.shape[1]), BF16),
        in_specs=[
            pl.BlockSpec(memory_space=pltpu.SMEM),
            pl.BlockSpec(memory_space=pltpu.VMEM),
            anywhere, anywhere, anywhere, anywhere,
        ],
        out_specs=pl.BlockSpec(memory_space=pltpu.VMEM),
        scratch_shapes=[
            pltpu.VMEM((rows, width), BF16),
            pltpu.VMEM(w_query.shape, BF16),
            pltpu.VMEM(w_out.shape, BF16),
            pltpu.VMEM((2, wide, tokens, features), BF16),
            pltpu.VMEM((rows, features), BF16),
            pltpu.VMEM((slots, features), BF16),
            pltpu.VMEM((slots, features), BF16),
            pltpu.VMEM((n, 8, CHUNK), F32),
            pltpu.VMEM((n, 8, CHUNK), F32),
            pltpu.VMEM((slots, features), BF16),
            pltpu.VMEM((slots, features), BF16),
            pltpu.VMEM((features, wide * tokens), BF16),
            pltpu.VMEM((rows, slots), BF16),
            pltpu.SemaphoreType.DMA((4,)),
            pltpu.SemaphoreType.DMA((2,)),
            pltpu.SemaphoreType.DMA((2,)),
            pltpu.SemaphoreType.DMA((n,)),
            pltpu.SemaphoreType.DMA((n,)),
            pltpu.SemaphoreType.DMA((n,)),
            pltpu.SemaphoreType.DMA((n,)),
            pltpu.SemaphoreType.DMA((n,)),
            pltpu.SemaphoreType.DMA((n,)),
        ],
        compiler_params=pltpu.CompilerParams(
            collective_id=0, has_side_effects=True, vmem_limit_bytes=48 * 1024 * 1024
        ),
        cost_estimate=pl.CostEstimate(
            flops=12 * 10**9, bytes_accessed=16 * 2**20, transcendentals=8 * 2**20
        ),
    )(slopes, info, new_rows, w_query, w_out, base_kv)


def solution(mesh):
    return jax.shard_map(
        functools.partial(per_device, mesh.shape["tm"]),
        mesh=mesh,
        in_specs=(
            P(("groups", "tm"), None),
            P(),
            P(),
            P(None, ("groups", "tm"), None, None),
            P(),
            P(("groups", "tm"), None),
            P(("groups", "tm")),
            P(("groups", "tm"), None),
        ),
        out_specs=P(("groups", "tm"), None),
        check_vma=False,
    )
```

```python
import functools

import jax
import jax.numpy as jnp
from jax import lax
from jax.experimental import pallas as pl
from jax.experimental.pallas import tpu as pltpu
from jax.sharding import PartitionSpec as P

HEAD_DIM = 128
REACH = 2
CHUNK = 128
MESH = pl.DeviceIdType.MESH
F32 = jnp.float32
BF16 = jnp.bfloat16


def iota(shape, axis):
    return lax.broadcasted_iota(jnp.int32, shape, axis)


def kernel(
    n, slopes_ref, info_ref, x_hbm, wq_hbm, wo_hbm, kv_hbm, out_hbm,
    x, wq, wo, ext, queries, q_slots, q_recv, m_slots, m_recv, att, ret, vt, gather, out,
    load_sem, wq_sem, out_sem, halo_send, halo_recv, qs_sem, qr_sem, ms_sem, mr_sem, rs_sem, rr_sem,
):
    me = lax.axis_index("tm")
    rows = x.shape[0]
    slots = q_slots.shape[0]
    cap = slots // n
    group = CHUNK // cap
    chunks = slots // CHUNK
    half = chunks // 2
    frames = kv_hbm.shape[1]
    wide = frames + 2 * REACH
    tokens = kv_hbm.shape[2]
    heads = queries.shape[1] // HEAD_DIM
    own = lax.div(me, group)
    own_half = lax.div(own, half)
    own_spot = lax.rem(own, half)

    barrier = pltpu.get_barrier_semaphore()

    @pl.loop(1, n)
    def _(k):
        pl.semaphore_signal(
            barrier, inc=1, device_id={"tm": lax.rem(me + k, n)}, device_id_type=MESH
        )

    load_x = pltpu.make_async_copy(x_hbm, x, load_sem.at[0])
    load_kv = pltpu.make_async_copy(kv_hbm, ext.at[:, REACH:REACH + frames], load_sem.at[1])
    load_wo = pltpu.make_async_copy(wo_hbm, wo, load_sem.at[2])

    def load_wq(j):
        columns = pl.ds(pl.multiple_of(j * 256, 256), 256)
        return pltpu.make_async_copy(wq_hbm.at[:, columns], wq.at[:, columns], wq_sem.at[j])

    load_x.start()

    @pl.loop(0, wq.shape[1] // 256)
    def _(j):
        load_wq(j).start()

    pl.semaphore_wait(barrier, n - 1)

    to_right = pltpu.make_async_remote_copy(
        src_ref=kv_hbm.at[:, frames - REACH:], dst_ref=ext.at[:, :REACH],
        send_sem=halo_send.at[0], recv_sem=halo_recv.at[0],
        device_id={"tm": lax.rem(me + 1, n)}, device_id_type=MESH,
    )
    to_left = pltpu.make_async_remote_copy(
        src_ref=kv_hbm.at[:, :REACH], dst_ref=ext.at[:, REACH + frames:],
        send_sem=halo_send.at[1], recv_sem=halo_recv.at[1],
        device_id={"tm": lax.rem(me + n - 1, n)}, device_id_type=MESH,
    )

    @pl.when(me < n - 1)
    def _():
        to_right.start()

    @pl.when(me > 0)
    def _():
        to_left.start()

    load_kv.start()
    edge = jnp.zeros((2, REACH, tokens, ext.shape[3]), BF16)

    @pl.when(me == 0)
    def _():
        ext[:, :REACH] = edge

    @pl.when(me == n - 1)
    def _():
        ext[:, REACH + frames:] = edge

    info = info_ref[...]
    owner = info[0:1]
    hits = (owner == iota((n, rows), 0).astype(F32)).astype(F32)
    upper = (iota((rows, rows), 0) <= iota((rows, rows), 1)).astype(F32).astype(BF16)
    counts = jnp.dot(hits.astype(BF16), upper, preferred_element_type=F32)
    rank = jnp.sum(hits * counts, axis=0, keepdims=True) - 1.0
    slot = owner * float(cap) + rank
    slot_column = jnp.sum(
        jnp.where(iota((rows, rows), 0) == iota((rows, rows), 1), slot, 0.0), axis=1, keepdims=True
    )
    gather[...] = (slot_column == iota((rows, slots), 1).astype(F32)).astype(F32).astype(BF16)
    facts = info.astype(BF16)
    spot = rank + (lax.rem(me, group) * cap).astype(F32)

    load_x.wait()

    @pl.loop(0, queries.shape[1] // 256)
    def _(j):
        load_wq(j).wait()
        columns = pl.ds(pl.multiple_of(j * 256, 256), 256)
        queries[:, columns] = jnp.dot(x[...], wq[:, columns], preferred_element_type=F32).astype(BF16)

    def q_copy(target, source):
        return pltpu.make_async_remote_copy(
            src_ref=q_slots.at[pl.ds(pl.multiple_of(target * cap, cap), cap)],
            dst_ref=q_recv.at[pl.ds(pl.multiple_of(source * cap, cap), cap)],
            send_sem=qs_sem.at[target], recv_sem=qr_sem.at[source],
            device_id={"tm": target}, device_id_type=MESH,
        )

    def m_copy(target, source):
        return pltpu.make_async_remote_copy(
            src_ref=m_slots.at[target], dst_ref=m_recv.at[source],
            send_sem=ms_sem.at[target], recv_sem=mr_sem.at[source],
            device_id={"tm": target}, device_id_type=MESH,
        )

    def r_copy(target, source):
        return pltpu.make_async_remote_copy(
            src_ref=att.at[pl.ds(pl.multiple_of(target * cap, cap), cap)],
            dst_ref=ret.at[pl.ds(pl.multiple_of(source * cap, cap), cap)],
            send_sem=rs_sem.at[target], recv_sem=rr_sem.at[source],
            device_id={"tm": target}, device_id_type=MESH,
        )

    mine = pl.ds(pl.multiple_of(me * cap, cap), cap)

    @pl.loop(0, chunks)
    def _(i):
        side = lax.rem(own_half + 1 + lax.div(i, half), 2)
        chunk = side * half + lax.rem(own_spot + lax.rem(i, half), half)
        first = (chunk * CHUNK).astype(F32)
        place = (slot - first == iota((CHUNK, rows), 0).astype(F32)).astype(F32).astype(BF16)

        @pl.loop(0, queries.shape[1] // 256)
        def _(j):
            columns = pl.ds(pl.multiple_of(j * 256, 256), 256)
            q_slots[pl.ds(pl.multiple_of(chunk * CHUNK, CHUNK), CHUNK), columns] = jnp.dot(
                place, queries[:, columns], preferred_element_type=F32
            ).astype(BF16)

        @pl.loop(0, group)
        def _(g):
            target = chunk * group + g
            lanes = jnp.where(owner == target.astype(F32), spot, -1.0)
            spread = (lanes == iota((CHUNK, rows), 0).astype(F32)).astype(F32).astype(BF16)
            m_slots[target] = lax.dot_general(
                facts, spread, (((1,), (1,)), ((), ())), preferred_element_type=F32
            )

            @pl.when(target != me)
            def _():
                m_copy(target, me).start()
                q_copy(target, me).start()

            @pl.when(target == me)
            def _():
                m_recv[target] = m_slots[target]
                q_recv[mine] = q_slots[mine]

    def turn(f):
        @pl.loop(0, heads)
        def _(h):
            columns = pl.ds(pl.multiple_of(h * HEAD_DIM, HEAD_DIM), HEAD_DIM)
            vt[columns, pl.ds(pl.multiple_of(f * tokens, tokens), tokens)] = (
                ext[1, f, :, columns].astype(F32).T.astype(BF16)
            )

    load_wo.start()
    load_kv.wait()

    @pl.loop(REACH, REACH + frames)
    def _(f):
        turn(f)

    @pl.when(me > 0)
    def _():
        to_right.wait_recv()

    @pl.when(me < n - 1)
    def _():
        to_left.wait_recv()

    @pl.loop(0, REACH)
    def _(f):
        turn(f)
        turn(REACH + frames + f)

    first_frame = (me * frames - REACH).astype(F32)

    @pl.loop(0, chunks)
    def _(i):
        side = lax.rem(own_half + lax.rem(i, 2), 2)
        chunk = side * half + lax.rem(own_spot + half - lax.div(i, 2), half)

        @pl.loop(0, group)
        def _(g):
            source = chunk * group + g

            @pl.when(source != me)
            def _():
                m_copy(me, source).wait_recv()
                q_copy(me, source).wait_recv()

        told = m_recv[chunk * group]
        for g in range(1, group):
            told = told + m_recv[chunk * group + g]
        position = told[1:2].astype(jnp.int32)
        ahead = lax.div(position, 3)
        centre = (ahead + REACH).astype(F32) + first_frame
        moment = centre + (position - 3 * ahead + 1).astype(F32) * 0.25
        frame = first_frame + iota((wide, CHUNK), 0).astype(F32)
        allowed = (frame >= centre - told[2:3]) & (frame <= centre + told[3:4])
        allowed = allowed & (frame >= 0.0) & (frame < float(frames * n))
        distance = jnp.abs(frame - moment)
        chunk_rows = pl.ds(pl.multiple_of(chunk * CHUNK, CHUNK), CHUNK)

        @pl.loop(0, heads, unroll=2)
        def _(h):
            columns = pl.ds(pl.multiple_of(h * HEAD_DIM, HEAD_DIM), HEAD_DIM)
            bias = jnp.where(allowed, -slopes_ref[h] * distance, -1e30)
            keys = ext[0, :, :, columns].reshape(wide * tokens, HEAD_DIM)
            scores = lax.dot_general(
                keys, q_recv[chunk_rows, columns], (((1,), (1,)), ((), ())),
                preferred_element_type=F32,
            )
            scores = scores.reshape(wide, tokens, CHUNK) * (1.0 / HEAD_DIM**0.5) + bias[:, None, :]
            largest = jnp.max(jnp.max(scores, axis=0), axis=0, keepdims=True)
            raised = jnp.exp(scores - largest[None])
            total = jnp.sum(jnp.sum(raised, axis=0), axis=0, keepdims=True)
            weights = (raised * (1.0 / total)[None]).astype(BF16).reshape(wide * tokens, CHUNK)
            attended = jnp.dot(vt[columns, :], weights, preferred_element_type=F32)
            att[chunk_rows, columns] = attended.T.astype(BF16)

        @pl.loop(0, group)
        def _(g):
            source = chunk * group + g

            @pl.when(source != me)
            def _():
                r_copy(source, me).start()

            @pl.when(source == me)
            def _():
                ret[mine] = att[mine]

    queries[...] = jnp.zeros(queries.shape, BF16)

    @pl.loop(0, chunks)
    def _(i):
        side = lax.rem(own_half + lax.div(i, half), 2)
        chunk = side * half + lax.rem(own_spot + lax.rem(i, half), half)

        @pl.loop(0, group)
        def _(g):
            source = chunk * group + g

            @pl.when(source != me)
            def _():
                r_copy(me, source).wait_recv()

        chunk_rows = pl.ds(pl.multiple_of(chunk * CHUNK, CHUNK), CHUNK)
        for j in range(queries.shape[1] // 256):
            columns = pl.ds(j * 256, 256)
            queries[:, columns] += jnp.dot(
                gather[:, chunk_rows], ret[chunk_rows, columns], preferred_element_type=F32
            ).astype(BF16)

    load_wo.wait()

    def write(j):
        columns = pl.ds(pl.multiple_of(j * 256, 256), 256)
        return pltpu.make_async_copy(out.at[:, columns], out_hbm.at[:, columns], out_sem.at[j])

    @pl.loop(0, wo.shape[1] // 256)
    def _(j):
        columns = pl.ds(pl.multiple_of(j * 256, 256), 256)
        out[:, columns] = jnp.dot(
            queries[...], wo[:, columns], preferred_element_type=F32
        ).astype(BF16)
        write(j).start()

    @pl.loop(0, wo.shape[1] // 256)
    def _(j):
        write(j).wait()

    @pl.loop(1, n)
    def _(k):
        target = lax.rem(me + k, n)
        m_copy(target, me).wait_send()
        q_copy(target, me).wait_send()
        r_copy(target, me).wait_send()

    @pl.when(me < n - 1)
    def _():
        to_right.wait_send()

    @pl.when(me > 0)
    def _():
        to_left.wait_send()


def per_device(n, new_rows, w_query, w_out, base_kv, slopes, row_owner, row_position, row_reach):
    rows, width = new_rows.shape
    features = w_query.shape[1]
    slots = 2 * rows
    frames, tokens = base_kv.shape[1:3]
    wide = frames + 2 * REACH
    info = jnp.concatenate(
        [row_owner.T, row_position[None], row_reach.T, jnp.zeros((4, rows), jnp.int32)], axis=0
    ).astype(F32)
    anywhere = pl.BlockSpec(memory_space=pl.ANY)
    return pl.pallas_call(
        functools.partial(kernel, n),
        out_shape=jax.ShapeDtypeStruct((rows, w_out.shape[1]), BF16),
        in_specs=[
            pl.BlockSpec(memory_space=pltpu.SMEM),
            pl.BlockSpec(memory_space=pltpu.VMEM),
            anywhere, anywhere, anywhere, anywhere,
        ],
        out_specs=anywhere,
        scratch_shapes=[
            pltpu.VMEM((rows, width), BF16),
            pltpu.VMEM(w_query.shape, BF16),
            pltpu.VMEM(w_out.shape, BF16),
            pltpu.VMEM((2, wide, tokens, features), BF16),
            pltpu.VMEM((rows, features), BF16),
            pltpu.VMEM((slots, features), BF16),
            pltpu.VMEM((slots, features), BF16),
            pltpu.VMEM((n, 8, CHUNK), F32),
            pltpu.VMEM((n, 8, CHUNK), F32),
            pltpu.VMEM((slots, features), BF16),
            pltpu.VMEM((slots, features), BF16),
            pltpu.VMEM((features, wide * tokens), BF16),
            pltpu.VMEM((rows, slots), BF16),
            pltpu.VMEM((rows, w_out.shape[1]), BF16),
            pltpu.SemaphoreType.DMA((3,)),
            pltpu.SemaphoreType.DMA((features // 256,)),
            pltpu.SemaphoreType.DMA((w_out.shape[1] // 256,)),
            pltpu.SemaphoreType.DMA((2,)),
            pltpu.SemaphoreType.DMA((2,)),
            pltpu.SemaphoreType.DMA((n,)),
            pltpu.SemaphoreType.DMA((n,)),
            pltpu.SemaphoreType.DMA((n,)),
            pltpu.SemaphoreType.DMA((n,)),
            pltpu.SemaphoreType.DMA((n,)),
            pltpu.SemaphoreType.DMA((n,)),
        ],
        compiler_params=pltpu.CompilerParams(
            collective_id=0, has_side_effects=True, vmem_limit_bytes=48 * 1024 * 1024
        ),
        cost_estimate=pl.CostEstimate(
            flops=12 * 10**9, bytes_accessed=16 * 2**20, transcendentals=8 * 2**20
        ),
    )(slopes, info, new_rows, w_query, w_out, base_kv)


def solution(mesh):
    return jax.shard_map(
        functools.partial(per_device, mesh.shape["tm"]),
        mesh=mesh,
        in_specs=(
            P(("groups", "tm"), None),
            P(),
            P(),
            P(None, ("groups", "tm"), None, None),
            P(),
            P(("groups", "tm"), None),
            P(("groups", "tm")),
            P(("groups", "tm"), None),
        ),
        out_specs=P(("groups", "tm"), None),
        check_vma=False,
    )
```
